32 devices in a mesh: seq: 4 (over z), tp: 4 (over y, x), lat: 2 (over core).
Axes of the slice: x: 2, y: 2, z: 4, core: 2. Of those that a mesh axis runs over, the one named last changes fastest.
Arguments:
- tokens: bfloat16 [3072, 8192], P(('seq', 'lat'), 'tp'), may hold values from -6 to 6
- active: int32 [3072, 4], P(('seq', 'lat')), may hold values from 0 to 31, all different within a row; in each aligned block of 384 rows (0 to 383, 384 to 767, ...) at most 72 rows name the same one
- placement_map: int32 [32], replicated, may hold values from 0 to 31, each once
- enc_weight: bfloat16 [8192, 4096], P('tp', ('seq', 'lat')), may hold values from -0.0625 to 0.0625
- enc_bias: float32 [4096], P(('seq', 'lat')), may hold values from -3 to 3
- dec_weight: bfloat16 [4096, 8192], P(('seq', 'lat'), 'tp'), may hold values from -0.375 to 0.375
- dec_bias: float32 [8192], P('tp'), may hold values from -3 to 3
Outputs:
- recon: bfloat16 [3072, 8192], P(('seq', 'lat'), 'tp')
The draws below stay inside these ranges and needn't reach their ends.
Inputs may be any that keep to these rules, and one draw needn't show every extreme that they name: `active`: the 4 blocks of one token are different. Among the rows of one device (aligned blocks of 384 rows) no block is named more than 72 times, and some block is named exactly 72 times. `placement_map`: each column block appears once.
All inputs are finite; a program needn't handle non-finite values.
Results may differ from the reference program's by a relative error of at most 0.0061.
Values may be sent and summed in bfloat16 or wider, within the bound.
No kernel may reach another device: no remote copies, remote signals or barrier semaphores. Data moves between devices by JAX's collectives and lax.ppermute only.
A program may use at most 128 MiB of HBM per device.

```python
import math
import jax
import jax.numpy as jnp
import numpy as np
from jax import lax

D = 8192
BLKW = 128
K = 4
TOK_DEV = 384
NBLK = 32
LATENTS = 4096
TOKENS = 3072
CAP = 72
N_SEQ = 4
N_LAT = 2


def steps_of(key, extent, split, least, largest):
    def one(dim, parts):
        heights = jax.random.uniform(jax.random.fold_in(jax.random.fold_in(key, 6), dim), (parts,), jnp.float32, least / len(split), largest / len(split))
        return jnp.repeat(jnp.exp(heights), extent[dim] // parts).reshape((-1,) + (1,) * (len(extent) - dim - 1))

    loudness = one(*split[0])
    for cut in split[1:]:
        loudness = loudness * one(*cut)
    return loudness


def assign_block(rng, own, number, rows, number_of, top, reach, lean):
    ranking = jax.random.permutation(rng, number_of)
    crowded, usual = portions_of(number_of, rows * top, reach, lean, True), portions_of(number_of, rows * top, reach, lean, False)
    places = jnp.arange(number_of)

    def named(tallies, turn):
        used = int((tallies > 0).sum())
        fixed = max(1, used // 4)
        passed = fixed + (places - fixed + turn * (used - fixed)) % max(1, number_of - fixed)
        return jnp.zeros((number_of,), jnp.int32).at[ranking[jnp.where(places < fixed, places, passed)]].set(jnp.asarray(tallies, jnp.int32))

    tallies = jnp.where(number % 4 == 0, named(crowded, number // 4), named(usual, number - number // 4 - 1))
    mixed = jax.random.permutation(jax.random.fold_in(own, 3), number_of)
    giver, sink = mixed[0:number_of // 2 * 2:2], mixed[1:number_of // 2 * 2:2]
    room = jnp.minimum(tallies[giver] - 1, reach - tallies[sink]) // 2
    room = jnp.where((giver == ranking[0]) | (sink == ranking[0]) | (tallies[sink] == 0), 0, jnp.maximum(room, 0))
    passed = jax.random.randint(jax.random.fold_in(own, 4), (number_of // 2,), 0, 1 << 20) % (room + 1)
    tallies = tallies.at[giver].add(-passed).at[sink].add(passed)
    labels = jnp.searchsorted(jnp.cumsum(tallies), jnp.arange(rows * top), side="right").astype(jnp.int32)
    table = labels.reshape(top, rows).T
    table = table[jax.random.permutation(jax.random.fold_in(own, 1), rows)]
    turn = jax.random.randint(jax.random.fold_in(own, 2), (rows, 1), 0, top)
    return jnp.take_along_axis(table, (jnp.arange(top)[None, :] + turn) % top, axis=1)


def portions_of(count, total, reach, slope, full):
    loads = [(1 << 20) // math.isqrt(grade ** slope) + 1 for grade in range(1, count + 1)]
    largest = reach if full else min(reach, max(-(-total // count), total * loads[0] // sum(loads)))
    least = 1 if total - largest >= count - 1 else 0
    counts, spare = [largest] + [least] * (count - 1), total - largest - least * (count - 1)
    while spare > 0:
        candidates = [i for i in range(1, count) if counts[i] < largest] or [i for i in range(1, count) if counts[i] < reach]
        whole, budget = sum([loads[i] for i in candidates]), spare
        for i in candidates:
            extra = min(reach - counts[i], max(1, budget * loads[i] // whole), spare)
            counts[i] = counts[i] + extra
            spare = spare - extra
    return np.array(counts)


def bell_draw(rng, extent, deviation, reach, split=(), kind=jnp.bfloat16):
    entries = jax.random.normal(rng, extent, jnp.float32) * deviation
    if len(split) > 0:
        entries = steps_of(rng, extent, split, -0.22, 0.18) * entries
    return jnp.clip(entries, min=-reach, max=reach).astype(kind)


def setup_inputs(seed: int = 0) -> dict:
    seeds = jax.random.split(jax.random.key(seed), 8)
    tokens = bell_draw(seeds[0], (TOKENS, D), 1.0, 6.0, ((0, 8), (1, 4)))
    active_keys = jax.random.split(jax.random.fold_in(seeds[1], 1), TOKENS // TOK_DEV)
    active_turns = jax.random.permutation(jax.random.fold_in(seeds[1], 3), TOKENS // TOK_DEV)
    active = jax.vmap(lambda own, number: assign_block(jax.random.fold_in(seeds[1], 2), own, number, TOK_DEV, NBLK, K, CAP, 2))(active_keys, active_turns).reshape((TOKENS, K))
    placement_map = jax.random.permutation(seeds[2], NBLK).astype(jnp.int32)
    enc_weight = bell_draw(seeds[3], (D, LATENTS), D ** -0.5, 0.0625, ((0, 4), (1, 8)))
    enc_bias = bell_draw(seeds[4], (LATENTS,), 0.5, 3.0, ((0, 8),), jnp.float32)
    dec_weight = bell_draw(seeds[5], (LATENTS, D), (K * BLKW // 2) ** -0.5, 0.375, ((0, 8), (1, 4)))
    dec_bias = bell_draw(seeds[6], (D,), 0.5, 3.0, ((0, 4),), jnp.float32)
    return {"tokens": tokens, "active": active, "placement_map": placement_map, "enc_weight": enc_weight, "enc_bias": enc_bias, "dec_weight": dec_weight, "dec_bias": dec_bias}


def reference(tokens, active, placement_map, enc_weight, enc_bias, dec_weight, dec_bias):
    centered = (tokens.astype(jnp.float32) - dec_bias[None, :]).astype(jnp.bfloat16)
    padded = jnp.concatenate([centered, jnp.zeros((1, D), jnp.bfloat16)], axis=0)
    position = placement_map[active].astype(jnp.int32)
    flat = position.reshape(-1)
    pair_row = (jnp.arange(TOKENS * K, dtype=jnp.int32) // K).astype(jnp.int32)
    hot = (flat[:, None] == jnp.arange(NBLK, dtype=jnp.int32)[None, :]).astype(jnp.int32)
    rank = jnp.sum((jnp.cumsum(hot, axis=0) - 1) * hot, axis=1).astype(jnp.int32)
    depth = N_SEQ * N_LAT * CAP
    table = jnp.full((NBLK, depth), TOKENS, jnp.int32).at[flat, rank].set(pair_row)

    def one_block(total, block):
        index = table[block]
        gathered = padded[index]
        start = (block * BLKW).astype(jnp.int32)
        w_enc = lax.dynamic_slice_in_dim(enc_weight, start, BLKW, 1)
        b_enc = lax.dynamic_slice_in_dim(enc_bias, start, BLKW, 0)
        preact = jnp.dot(gathered, w_enc, preferred_element_type=jnp.float32) + b_enc[None, :]
        codes = jnp.maximum(preact, 0.0).astype(jnp.bfloat16)
        w_dec = lax.dynamic_slice_in_dim(dec_weight, start, BLKW, 0)
        part = jnp.dot(codes, w_dec, preferred_element_type=jnp.float32).astype(jnp.bfloat16)
        total = total.at[index].add(part.astype(jnp.float32))
        return total, None

    total = jnp.zeros((TOKENS + 1, D), jnp.float32)
    total, _ = lax.scan(one_block, total, jnp.arange(NBLK, dtype=jnp.int32))
    return (total[:TOKENS] + dec_bias[None, :]).astype(jnp.bfloat16)
```

```python
import jax
import jax.numpy as jnp
from jax import lax
from jax.sharding import PartitionSpec as P

CH = 4
TO_MID = [(0, 1), (3, 2)]
ACROSS = [(1, 2), (2, 1)]
TO_END = [(1, 0), (2, 3)]
BF = jnp.bfloat16


def line(tokens, active, placement_map, enc_weight, enc_bias, dec_weight, dec_bias):
    rows, width = tokens.shape
    top = active.shape[1]
    nblocks = placement_map.shape[0]
    nseq, nlat = lax.axis_size("seq"), lax.axis_size("lat")
    local_blocks = nblocks // (nseq * nlat)
    bw = enc_bias.shape[0] // local_blocks
    s, l = lax.axis_index("seq"), lax.axis_index("lat")
    end = (s == 0) | (s == nseq - 1)
    r = rows // CH
    pp = lax.ppermute
    centered = (tokens.astype(jnp.float32) - dec_bias[None, :]).astype(BF)
    swap = [(0, 1), (1, 0)]
    act_all = lax.all_gather(active, "seq", axis=0)
    table = jnp.array([[0, 1, 2, 3], [1, 2, 3, 0], [2, 1, 0, 3], [3, 2, 1, 0]], jnp.int32)
    src = table[s]
    act = jnp.stack([lax.dynamic_index_in_dim(act_all, src[i], 0, False) for i in range(4)])
    act = act.reshape(4, CH, r, top).swapaxes(0, 1)
    base = (s * nlat + l) * local_blocks
    obase = (s * nlat + (1 - l)) * local_blocks
    ids = jnp.arange(nblocks, dtype=jnp.int32)
    inv = jnp.sum(jnp.where(placement_map[None, :] == ids[:, None], ids[None, :], 0), axis=1)
    mine = jnp.concatenate([lax.dynamic_slice_in_dim(inv, base, local_blocks), lax.dynamic_slice_in_dim(inv, obase, local_blocks)])
    nb = 2 * local_blocks
    enc_o = pp(enc_weight, "lat", swap)
    dec_o = pp(dec_weight, "lat", swap)
    bias = jnp.concatenate([enc_bias, pp(enc_bias, "lat", swap)]).reshape(nb, bw)

    outs = []
    for c in range(CH):
        x = centered[c * r:(c + 1) * r]
        ac1 = pp(x, "seq", TO_MID + TO_END)
        b1 = pp(x, "seq", ACROSS)
        b2 = pp(ac1, "seq", ACROSS)
        c2 = pp(b1, "seq", TO_END)
        c3 = pp(b2, "seq", TO_END)
        xs = jnp.concatenate([x, jnp.where(end, ac1, b1), jnp.where(end, c2, b2), jnp.where(end, c3, ac1)])
        pre = jnp.concatenate([
            jnp.dot(xs, enc_weight, preferred_element_type=jnp.float32),
            jnp.dot(xs, enc_o, preferred_element_type=jnp.float32)], axis=1).reshape(4 * r, nb, bw)
        hit = act[c].reshape(4 * r, top)[:, :, None] == mine[None, None, :]
        part = jnp.concatenate([
            sum(jnp.where(hit[:, k, b, None], pre[:, b], 0.0) for b in range(nb)) for k in range(top)], axis=1)
        pb = part.astype(BF)
        tot = part + (pp(pb, "tp", [(0, 1), (1, 0), (2, 3), (3, 2)]).astype(jnp.float32)
                      + pp(pb, "tp", [(0, 2), (2, 0), (1, 3), (3, 1)]).astype(jnp.float32)
                      + pp(pb, "tp", [(0, 3), (3, 0), (1, 2), (2, 1)]).astype(jnp.float32))
        tot = tot.reshape(4 * r, top, bw)
        codes = jnp.concatenate([
            sum(jnp.where(hit[:, k, b, None], jnp.maximum(tot[:, k] + bias[b][None, :], 0.0), 0.0) for k in range(top))
            for b in range(nb)], axis=1).astype(BF)
        h = local_blocks * bw
        y = (jnp.dot(codes[:, :h], dec_weight, preferred_element_type=jnp.float32)
             + jnp.dot(codes[:, h:], dec_o, preferred_element_type=jnp.float32))
        y0, y1, y2, y3 = y[:r], y[r:2 * r], y[2 * r:3 * r], y[3 * r:]
        f32 = lambda z: z.astype(jnp.float32)
        a3 = pp(y3.astype(BF), "seq", TO_MID)
        m2 = (y2 + f32(a3)).astype(BF)
        a2 = pp(m2, "seq", TO_MID)
        rb2 = pp(m2, "seq", ACROSS)
        m1 = (y1 + f32(a2)).astype(BF)
        rb1 = pp(m1, "seq", ACROSS)
        ac = pp(jnp.where(end, m1, (y3 + f32(rb2)).astype(BF)), "seq", TO_MID + TO_END)
        outs.append((y0 + f32(ac) + f32(rb1) + dec_bias[None, :]).astype(BF))
    return jnp.concatenate(outs)


def general(tokens, active, placement_map, enc_weight, enc_bias, dec_weight, dec_bias):
    rows, width = tokens.shape
    top = active.shape[1]
    nblocks = placement_map.shape[0]
    seq_count = lax.axis_size("seq")
    lat_count = lax.axis_size("lat")
    owners = seq_count * lat_count
    local_blocks = nblocks // owners
    block_width = enc_bias.shape[0] // local_blocks
    capacity = 3 * rows * top // (2 * nblocks)
    centered = (tokens.astype(jnp.float32) - dec_bias[None, :]).astype(jnp.bfloat16)
    block_ids = jnp.arange(nblocks, dtype=jnp.int32)
    matches = (active[:, :, None] == block_ids[None, None, :]).astype(jnp.int32)
    position = jnp.sum(matches * placement_map[None, None, :], axis=2).reshape(-1)
    pos_hot = (position[:, None] == block_ids[None, :]).astype(jnp.int32)
    rank = jnp.sum((jnp.cumsum(pos_hot, axis=0) - 1) * pos_hot, axis=1)
    target = position * capacity + rank
    pair_row = jnp.arange(rows * top, dtype=jnp.int32) // top
    slot_row = jnp.zeros((nblocks * capacity,), jnp.int32).at[target].set(pair_row)
    filled = jnp.zeros((nblocks * capacity,), jnp.bool_).at[target].set(True)
    outgoing = jnp.where(filled[:, None], centered[slot_row], jnp.zeros((), jnp.bfloat16))
    outgoing = outgoing.reshape(owners, local_blocks, capacity, width)
    enc_blocks = enc_weight.reshape(width, local_blocks, block_width)
    bias_blocks = enc_bias.reshape(local_blocks, block_width)
    dec_blocks = dec_weight.reshape(local_blocks, block_width, width)
    preact = jnp.einsum(
        "sbcd,dbh->sbch",
        lax.all_to_all(outgoing, ("seq", "lat"), split_axis=0, concat_axis=0, tiled=True),
        enc_blocks,
        preferred_element_type=jnp.float32,
    )
    summed = lax.psum(preact, "tp")
    codes = jnp.maximum(summed + bias_blocks[None, :, None, :], 0.0).astype(jnp.bfloat16)
    returned = lax.all_to_all(
        jnp.einsum("sbch,bhd->sbcd", codes, dec_blocks, preferred_element_type=jnp.float32).astype(
            jnp.bfloat16
        ),
        ("seq", "lat"),
        split_axis=0,
        concat_axis=0,
        tiled=True,
    )
    returned = returned.reshape(nblocks * capacity, width)
    contrib = returned[target].reshape(rows, top, width).astype(jnp.float32)
    return (jnp.sum(contrib, axis=1) + dec_bias[None, :]).astype(jnp.bfloat16)


def solution(mesh):
    return jax.shard_map(
        line if dict(mesh.shape) == {"seq": 4, "tp": 4, "lat": 2} else general,
        mesh=mesh,
        in_specs=(
            P(("seq", "lat"), "tp"),
            P(("seq", "lat"), None),
            P(),
            P("tp", ("seq", "lat")),
            P(("seq", "lat")),
            P(("seq", "lat"), "tp"),
            P("tp"),
        ),
        out_specs=P(("seq", "lat"), "tp"),
        check_vma=False,
    )
```

```python
import jax
import jax.numpy as jnp
from jax import lax
from jax.experimental import pallas as pl
from jax.experimental.pallas import tpu as pltpu
from jax.sharding import PartitionSpec as P

SIXTHS = (12, 12)
ORDER = (
    "named.0", "x.0", "all.0", "b1.0", "setup.0", "x.1", "wa1.0", "b2.0", "b1.1", "a1.1", "c2.0",
    "ena.0", "c3.0", "c1.1", "b2.1", "wc2.0", "c2.1", "dea.0", "wc3.0", "s1.0", "enb.0", "wb2.1",
    "wc1.1", "c3.1", "ena.1", "ws1.0", "wc2.1", "deb.0", "s3.0", "s2.0", "dea.1", "wc3.1", "s1.1",
    "enb.1", "t2.0", "t1.0", "deb.1", "s3.1", "wt2.0", "ws1.1", "u1.0", "s2.1", "wt1.0", "t2.1",
    "fin.0", "t1.1", "u1.1", "wt1.1", "fin.1",
)
TO_MID = [(0, 1), (3, 2)]
ACROSS = [(1, 2), (2, 1)]
TO_END = [(1, 0), (2, 3)]
SWAP = [(0, 1), (1, 0)]
BF = jnp.bfloat16
F32 = jnp.float32
WSPEC = pl.BlockSpec(memory_space=pltpu.VMEM)
VMEM = 20 << 20
DTILE = 1024
ONEAR = True


def encode_kernel(slots, off, s_ref, pos, *refs):
    half = len(slots)
    at_end, at_mid = refs[:half], refs[half:2 * half]
    wo, wp, out, xs, pre, sem = refs[2 * half:]
    r = out.shape[0] // half
    top = pos.shape[2]
    bw = out.shape[1] // top
    cols = wo.shape[1]
    end = s_ref[0] == 1

    def move(i, src):
        return pltpu.make_async_copy(src, xs.at[i * r:(i + 1) * r], sem.at[i])

    @pl.when(end)
    def _():
        for i, src in enumerate(at_end):
            move(i, src).start()

    @pl.when(jnp.logical_not(end))
    def _():
        for i, src in enumerate(at_mid):
            move(i, src).start()

    for i in range(half):
        move(i, at_end[i]).wait()
    pre[:, :cols] = jnp.dot(xs[...], wo[...], preferred_element_type=F32)
    pre[:, cols:] = jnp.dot(xs[...], wp[...], preferred_element_type=F32)
    step = next(n for n in (64, 48, 32, 16) if r % n == 0)
    for i, slot in enumerate(slots):
        for at in range(0, r, step):
            p = pos[s_ref[3 + slot], off + at:off + at + step, :]
            rs = slice(i * r + at, i * r + at + step)
            for k in range(top):
                q = jnp.broadcast_to(p[:, k:k + 1], (step, bw))
                a = jnp.zeros((step, bw), F32)
                for b in range(2 * cols // bw):
                    base = s_ref[1] + b if b < cols // bw else s_ref[2] + b - cols // bw
                    a = jnp.where(q == base, pre[rs, b * bw:(b + 1) * bw], a)
                out[rs, k * bw:(k + 1) * bw] = a.astype(BF)


def decode_kernel(slots, off, s_ref, pos, own, px, py, pd, bo, bp, wo, wp, *refs):
    outs, codes = refs[:-1], refs[-1]
    top = pos.shape[2]
    bw = own.shape[1] // top
    r = outs[0].shape[0]
    h, width = wo.shape
    for i, slot in enumerate(slots):
        p = pos[s_ref[3 + slot], off:off + r, :]
        rs = slice(i * r, (i + 1) * r)
        wide = [jnp.broadcast_to(p[:, k:k + 1], (r, bw)) for k in range(top)]
        tot = [own[rs, c].astype(F32) + px[rs, c].astype(F32) + (py[rs, c].astype(F32) + pd[rs, c].astype(F32))
               for c in (slice(k * bw, (k + 1) * bw) for k in range(top))]
        for bias, base, at in ((bo, s_ref[1], 0), (bp, s_ref[2], h)):
            for b in range(h // bw):
                v = jnp.full((r, bw), -jnp.inf, F32)
                for k in range(top):
                    v = jnp.where(wide[k] == base + b, tot[k], v)
                codes[rs, at + b * bw:at + (b + 1) * bw] = jnp.maximum(v + bias[:, b * bw:(b + 1) * bw], 0.0).astype(BF)
    tile = DTILE
    for n in range(width // tile):
        c = slice(n * tile, (n + 1) * tile)
        y = jnp.dot(codes[:, :h], wo[:, c], preferred_element_type=F32) + jnp.dot(
            codes[:, h:], wp[:, c], preferred_element_type=F32)
        for i, o in enumerate(outs):
            o[:, c] = y[i * r:(i + 1) * r].astype(o.dtype)


NEAR, FAR = pl.BlockSpec(memory_space=pltpu.VMEM), pl.BlockSpec(memory_space=pl.ANY)


def encode(scal, pos, off, slots, at_end, at_mid, wo, wp, bw):
    r, width = at_end[0].shape
    cols = wo.shape[1]
    top = pos.shape[2]
    n = len(slots)
    return pl.pallas_call(
        lambda *refs: encode_kernel(slots, off, *refs),
        out_shape=jax.ShapeDtypeStruct((n * r, top * bw), BF),
        in_specs=[pl.BlockSpec(memory_space=pltpu.SMEM), NEAR] + [FAR] * (2 * n) + [WSPEC] * 2,
        out_specs=NEAR if ONEAR else FAR,
        scratch_shapes=[pltpu.VMEM((n * r, width), BF), pltpu.VMEM((n * r, 2 * cols), F32), pltpu.SemaphoreType.DMA((n,))],
        compiler_params=pltpu.CompilerParams(vmem_limit_bytes=VMEM),
        cost_estimate=pl.CostEstimate(flops=1, bytes_accessed=1, transcendentals=0),
        name="encode",
    )(scal, pos, *at_end, *at_mid, wo, wp)


def decode(scal, pos, off, slots, kinds, parts, bo, bp, wo, wp):
    n = len(slots)
    r = parts[0].shape[0] // n
    half, width = wo.shape
    return pl.pallas_call(
        lambda *refs: decode_kernel(slots, off, *refs),
        out_shape=[jax.ShapeDtypeStruct((r, width), kind) for kind in kinds],
        in_specs=[pl.BlockSpec(memory_space=pltpu.SMEM)] + [NEAR] * 7 + [WSPEC] * 2,
        out_specs=[NEAR] * n,
        scratch_shapes=[pltpu.VMEM((n * r, 2 * half), BF)],
        compiler_params=pltpu.CompilerParams(vmem_limit_bytes=VMEM),
        cost_estimate=pl.CostEstimate(flops=1, bytes_accessed=1, transcendentals=0),
        name="decode",
    )(scal, pos, *parts, bo, bp, wo, wp)


def line(tokens, active, placement_map, enc_weight, enc_bias, dec_weight, dec_bias):
    rows, width = tokens.shape
    nblocks = placement_map.shape[0]
    nseq, nlat = lax.axis_size("seq"), lax.axis_size("lat")
    local_blocks = nblocks // (nseq * nlat)
    bw = enc_bias.shape[0] // local_blocks
    s, l = lax.axis_index("seq"), lax.axis_index("lat")
    chunks = len(SIXTHS)
    sizes = [rows * n // sum(SIXTHS) for n in SIXTHS]
    offs = [sum(sizes[:c]) for c in range(chunks)]
    pp = lax.ppermute
    f32 = lambda z: z.astype(F32)
    last = ()
    v = [dict() for _ in range(chunks)]
    m = {}
    at_end = (s == 0) | (s == nseq - 1)

    def after(*vals):
        if last:
            vals = lax.optimization_barrier(tuple(vals) + tuple(last))[:len(vals)]
        return vals

    def mark(*vals):
        nonlocal last
        last = vals

    def wait(d, *names):
        vals = after(*[d[n] for n in names])
        d.update(zip(names, vals))
        mark(*vals)

    def named():
        ids = jnp.arange(nblocks, dtype=jnp.int32)
        pos = jnp.sum(jnp.where(active[:, :, None] == ids, placement_map, 0), axis=2)
        m["n0"] = pos
        for k in range(1, nseq):
            m[f"n{k}"] = pp(pos, "seq", [(i, (i + k) % nseq) for i in range(nseq)])
        wait(m, *[f"n{k}" for k in range(1, nseq)])
        m["pos"] = jnp.stack([m[f"n{k}"] for k in range(nseq)])

    def setup():
        ew, dw = after(enc_weight, dec_weight)
        m["ep"] = pp(ew, "lat", SWAP)
        m["dp"] = pp(dw, "lat", SWAP)
        m["bo"] = enc_bias[None, :]
        m["bp"] = pp(m["bo"], "lat", SWAP)
        at = jnp.array([[0, 1, 2, 3], [1, 2, 3, 0], [2, 1, 0, 3], [3, 2, 1, 0]], jnp.int32)
        m["scal"] = jnp.concatenate([jnp.stack([at_end.astype(jnp.int32), (s * nlat + l) * local_blocks,
                                                (s * nlat + 1 - l) * local_blocks]), lax.rem(s - at[s] + nseq, nseq)])

    def step(name, c):
        d = v[c]
        if name == "x":
            (x,) = after(tokens[offs[c]:offs[c] + sizes[c]])
            d["x"] = (f32(x) - dec_bias[None, :]).astype(BF)
            mark(d["x"])
        elif name == "all":
            d["a1"] = d["c1"] = pp(after(d["x"])[0], "seq", TO_MID + TO_END)
        elif name == "setup":
            setup()
        elif name == "named":
            named()
        elif name == "a1":
            d["a1"] = pp(after(d["x"])[0], "seq", TO_MID)
        elif name == "b1":
            d["b1"] = pp(after(d["x"])[0], "seq", ACROSS)
        elif name == "c1":
            d["c1"] = pp(after(d["x"])[0], "seq", TO_END)
        elif name == "b2":
            wait(d, "a1")
            d["b2"] = pp(d["a1"], "seq", ACROSS)
        elif name == "c2":
            wait(d, "b1")
            d["c2"] = pp(d["b1"], "seq", TO_END)
        elif name == "c3":
            wait(d, "b2")
            d["c3"] = pp(d["b2"], "seq", TO_END)
        elif name in ("wxa", "wxb"):
            wait(d, *["p" + name[2] + n for n in ("d", "x", "y")])
        elif name[0] == "w":
            wait(d, name[1:])
        elif name in ("ena", "enb"):
            h = name[2]
            ends, mids, slots = (("x", "c1"), ("x", "b1"), (0, 1)) if h == "a" else (("c2", "c3"), ("b2", "a1"), (2, 3))
            rows = after(*[d[n] for n in ends + mids])
            pb = encode(m["scal"], m["pos"], offs[c], slots, rows[:2], rows[2:], enc_weight, m["ep"], bw)
            mark(pb)
            d["p" + h] = pb
            for n, p in (("d", [(0, 3), (3, 0), (1, 2), (2, 1)]), ("x", [(0, 1), (1, 0), (2, 3), (3, 2)]),
                         ("y", [(0, 2), (2, 0), (1, 3), (3, 1)])):
                d["p" + h + n] = pp(pb, "tp", p)
        elif name in ("dea", "deb"):
            h = name[2]
            parts = after(*[d["p" + h + n] for n in ("", "x", "y", "d")])
            slots, kinds, ys = ((0, 1), (F32, BF), ("y0", "y1")) if h == "a" else ((2, 3), (BF, BF), ("y2", "y3"))
            out = decode(m["scal"], m["pos"], offs[c], slots, kinds, parts, m["bo"], m["bp"], dec_weight, m["dp"])
            mark(*out)
            d.update(zip(ys, out))
        elif name in ("s3", "s2", "s1"):
            d[name] = pp(after(d["y" + name[1]])[0], "seq", TO_MID)
        elif name in ("t2", "t1"):
            wait(d, "s3" if name == "t2" else "s2")
            z = (f32(d["y" + name[1]]) + f32(d["s3" if name == "t2" else "s2"])).astype(BF)
            mark(z)
            d[name] = pp(z, "seq", ACROSS)
        elif name == "u1":
            wait(d, "t2")
            z = (f32(d["y3"]) + f32(d["t2"])).astype(BF)
            mark(z)
            d[name] = pp(z, "seq", TO_END)
        elif name == "fin":
            wait(d, "s1", "t1", "u1")
            d["out"] = (d["y0"] + (f32(d["s1"]) + f32(d["t1"]) + f32(d["u1"])) + dec_bias[None, :]).astype(BF)
            mark(d["out"])
        else:
            raise ValueError(name)

    for item in ORDER:
        name, c = item.split(".")
        step(name, int(c))
    return jnp.concatenate([d["out"] for d in v])


def general(tokens, active, placement_map, enc_weight, enc_bias, dec_weight, dec_bias):
    rows, width = tokens.shape
    top = active.shape[1]
    nblocks = placement_map.shape[0]
    seq_count = lax.axis_size("seq")
    lat_count = lax.axis_size("lat")
    owners = seq_count * lat_count
    local_blocks = nblocks // owners
    block_width = enc_bias.shape[0] // local_blocks
    capacity = 3 * rows * top // (2 * nblocks)
    centered = (tokens.astype(jnp.float32) - dec_bias[None, :]).astype(jnp.bfloat16)
    block_ids = jnp.arange(nblocks, dtype=jnp.int32)
    matches = (active[:, :, None] == block_ids[None, None, :]).astype(jnp.int32)
    position = jnp.sum(matches * placement_map[None, None, :], axis=2).reshape(-1)
    pos_hot = (position[:, None] == block_ids[None, :]).astype(jnp.int32)
    rank = jnp.sum((jnp.cumsum(pos_hot, axis=0) - 1) * pos_hot, axis=1)
    target = position * capacity + rank
    pair_row = jnp.arange(rows * top, dtype=jnp.int32) // top
    slot_row = jnp.zeros((nblocks * capacity,), jnp.int32).at[target].set(pair_row)
    filled = jnp.zeros((nblocks * capacity,), jnp.bool_).at[target].set(True)
    outgoing = jnp.where(filled[:, None], centered[slot_row], jnp.zeros((), jnp.bfloat16))
    outgoing = outgoing.reshape(owners, local_blocks, capacity, width)
    enc_blocks = enc_weight.reshape(width, local_blocks, block_width)
    bias_blocks = enc_bias.reshape(local_blocks, block_width)
    dec_blocks = dec_weight.reshape(local_blocks, block_width, width)
    preact = jnp.einsum(
        "sbcd,dbh->sbch",
        lax.all_to_all(outgoing, ("seq", "lat"), split_axis=0, concat_axis=0, tiled=True),
        enc_blocks,
        preferred_element_type=jnp.float32,
    )
    summed = lax.psum(preact, "tp")
    codes = jnp.maximum(summed + bias_blocks[None, :, None, :], 0.0).astype(jnp.bfloat16)
    returned = lax.all_to_all(
        jnp.einsum("sbch,bhd->sbcd", codes, dec_blocks, preferred_element_type=jnp.float32).astype(
            jnp.bfloat16
        ),
        ("seq", "lat"),
        split_axis=0,
        concat_axis=0,
        tiled=True,
    )
    returned = returned.reshape(nblocks * capacity, width)
    contrib = returned[target].reshape(rows, top, width).astype(jnp.float32)
    return (jnp.sum(contrib, axis=1) + dec_bias[None, :]).astype(jnp.bfloat16)


def solution(mesh):
    return jax.shard_map(
        line if dict(mesh.shape) == {"seq": 4, "tp": 4, "lat": 2} else general,
        mesh=mesh,
        in_specs=(
            P(("seq", "lat"), "tp"),
            P(("seq", "lat"), None),
            P(),
            P("tp", ("seq", "lat")),
            P(("seq", "lat")),
            P(("seq", "lat"), "tp"),
            P("tp"),
        ),
        out_specs=P(("seq", "lat"), "tp"),
        check_vma=False,
    )
```

```python
import jax
import jax.numpy as jnp
from jax import lax
from jax.experimental import pallas as pl
from jax.experimental.pallas import tpu as pltpu
from jax.sharding import PartitionSpec as P

SIXTHS = (12, 12)
DIRECT = ''
ORDER = (
    "x.0", "all.0", "b1.0", "x.1", "named.0", "wa1.0", "wb1.0", "b2.0", "c2.0", "setup.0", "wset.0",
    "a1.1", "b1.1", "ena.0", "c3.0", "wc2.0", "ma.0", "b2.1", "c1.1", "dea.0", "s1.0", "wc3.0",
    "enb.0", "c2.1", "mb.0", "wc1.1", "ena.1", "ws1.0", "c3.1", "deb.0", "s3.0", "s2.0", "wc2.1",
    "ma.1", "dea.1", "s1.1", "t2.0", "wc3.1", "enf.1", "t1.0", "u1.0", "mf.1", "wxf.1", "def.1",
    "s3p.1", "s2p.1", "s3q.1", "s2q.1", "ws1.1", "fin.0", "t2p.1", "t1p.1", "u1p.1", "t2q.1",
    "t1q.1", "u1q.1", "fin.1",
)
TO_MID = [(0, 1), (3, 2)]
ACROSS = [(1, 2), (2, 1)]
TO_END = [(1, 0), (2, 3)]
SWAP = [(0, 1), (1, 0)]
X_TP, Y_TP, FAR_TP = [(0, 1), (1, 0), (2, 3), (3, 2)], [(0, 2), (2, 0), (1, 3), (3, 1)], [(0, 3), (3, 0), (1, 2), (2, 1)]
BF = jnp.bfloat16
F32 = jnp.float32
WSPEC = pl.BlockSpec(memory_space=pltpu.VMEM)
VMEM = 20 << 20
DTILE = 1024
ONEAR = True


def encode_kernel(slots, off, s_ref, pos, *refs):
    half = len(slots)
    at_end, at_mid = refs[:half], refs[half:2 * half]
    wo, wp, out, xs, pre, sem = refs[2 * half:]
    r = out.shape[0] // half
    top = pos.shape[2]
    bw = out.shape[1] // top
    cols = wo.shape[1]
    end = s_ref[0] == 1

    def move(i, src):
        return pltpu.make_async_copy(src, xs.at[i * r:(i + 1) * r], sem.at[i])

    @pl.when(end)
    def _():
        for i, src in enumerate(at_end):
            move(i, src).start()

    @pl.when(jnp.logical_not(end))
    def _():
        for i, src in enumerate(at_mid):
            move(i, src).start()

    for i in range(half):
        move(i, at_end[i]).wait()
    pre[:, :cols] = jnp.dot(xs[...], wo[...], preferred_element_type=F32)
    pre[:, cols:] = jnp.dot(xs[...], wp[...], preferred_element_type=F32)
    step = next(n for n in (64, 48, 32, 16) if r % n == 0)
    for i, slot in enumerate(slots):
        for at in range(0, r, step):
            p = pos[s_ref[3 + slot], off + at:off + at + step, :]
            rs = slice(i * r + at, i * r + at + step)
            for k in range(top):
                q = jnp.broadcast_to(p[:, k:k + 1], (step, bw))
                a = jnp.zeros((step, bw), F32)
                for b in range(2 * cols // bw):
                    base = s_ref[1] + b if b < cols // bw else s_ref[2] + b - cols // bw
                    a = jnp.where(q == base, pre[rs, b * bw:(b + 1) * bw], a)
                out[rs, k * bw:(k + 1) * bw] = a.astype(BF)


def decode_kernel(slots, off, count, s_ref, pos, *refs):
    parts, (bo, bp, wo, wp), outs, codes = refs[:count], refs[count:count + 4], refs[count + 4:-1], refs[-1]
    own = parts[0]
    top = pos.shape[2]
    bw = own.shape[1] // top
    r = own.shape[0] // len(slots)
    h, width = wo.shape
    for i, slot in enumerate(slots):
        p = pos[s_ref[3 + slot], off:off + r, :]
        rs = slice(i * r, (i + 1) * r)
        wide = [jnp.broadcast_to(p[:, k:k + 1], (r, bw)) for k in range(top)]
        tot = [sum(p_[rs, c].astype(F32) for p_ in parts)
               for c in (slice(k * bw, (k + 1) * bw) for k in range(top))]
        for bias, base, at in ((bo, s_ref[1], 0), (bp, s_ref[2], h)):
            for b in range(h // bw):
                v = jnp.full((r, bw), -jnp.inf, F32)
                for k in range(top):
                    v = jnp.where(wide[k] == base + b, tot[k], v)
                codes[rs, at + b * bw:at + (b + 1) * bw] = jnp.maximum(v + bias[:, b * bw:(b + 1) * bw], 0.0).astype(BF)
    tile = DTILE
    for n in range(width // tile):
        c = slice(n * tile, (n + 1) * tile)
        y = jnp.dot(codes[:, :h], wo[:, c], preferred_element_type=F32) + jnp.dot(
            codes[:, h:], wp[:, c], preferred_element_type=F32)
        row = 0
        for o in outs:
            o[:, c] = y[row:row + o.shape[0]].astype(o.dtype)
            row += o.shape[0]


GROUPS = {
    "a": (("x", "c1"), ("x", "b1"), (0, 1), ("y0", "y1")),
    "b": (("c2", "c3"), ("b2", "a1"), (2, 3), ("y2", "y3")),
    "d": (("c2",), ("b2",), (2,), ("y2",)),
    "f": (("c2", "c3"), ("b2", "a1"), (2, 3), ("y2p", "y2q", "y3p", "y3q")),
    "e": (("c3",), ("a1",), (3,), ("y3p", "y3q")),
}
NEAR, FAR = pl.BlockSpec(memory_space=pltpu.VMEM), pl.BlockSpec(memory_space=pl.ANY)


def encode(scal, pos, off, slots, at_end, at_mid, wo, wp, bw):
    r, width = at_end[0].shape
    cols = wo.shape[1]
    top = pos.shape[2]
    n = len(slots)
    return pl.pallas_call(
        lambda *refs: encode_kernel(slots, off, *refs),
        out_shape=jax.ShapeDtypeStruct((n * r, top * bw), BF),
        in_specs=[pl.BlockSpec(memory_space=pltpu.SMEM), NEAR] + [FAR] * (2 * n) + [WSPEC] * 2,
        out_specs=NEAR if ONEAR else FAR,
        scratch_shapes=[pltpu.VMEM((n * r, width), BF), pltpu.VMEM((n * r, 2 * cols), F32), pltpu.SemaphoreType.DMA((n,))],
        compiler_params=pltpu.CompilerParams(vmem_limit_bytes=VMEM),
        cost_estimate=pl.CostEstimate(flops=1, bytes_accessed=1, transcendentals=0),
        name="encode",
    )(scal, pos, *at_end, *at_mid, wo, wp)


def decode(scal, pos, off, slots, kinds, parts, bo, bp, wo, wp, cut=1):
    n = len(slots)
    r = parts[0].shape[0] // n
    half, width = wo.shape
    return pl.pallas_call(
        lambda *refs: decode_kernel(slots, off, len(parts), *refs),
        out_shape=[jax.ShapeDtypeStruct((r // cut, width), kind) for kind in kinds for _ in range(cut)],
        in_specs=[pl.BlockSpec(memory_space=pltpu.SMEM)] + [NEAR] * (3 + len(parts)) + [WSPEC] * 2,
        out_specs=[NEAR] * (len(kinds) * cut),
        scratch_shapes=[pltpu.VMEM((n * r, 2 * half), BF)],
        compiler_params=pltpu.CompilerParams(vmem_limit_bytes=VMEM),
        cost_estimate=pl.CostEstimate(flops=1, bytes_accessed=1, transcendentals=0),
        name="decode",
    )(scal, pos, *parts, bo, bp, wo, wp)


def line(tokens, active, placement_map, enc_weight, enc_bias, dec_weight, dec_bias):
    rows, width = tokens.shape
    nblocks = placement_map.shape[0]
    nseq, nlat = lax.axis_size("seq"), lax.axis_size("lat")
    local_blocks = nblocks // (nseq * nlat)
    bw = enc_bias.shape[0] // local_blocks
    s, l = lax.axis_index("seq"), lax.axis_index("lat")
    chunks = len(SIXTHS)
    sizes = [rows * n // sum(SIXTHS) for n in SIXTHS]
    offs = [sum(sizes[:c]) for c in range(chunks)]
    pp = lax.ppermute
    f32 = lambda z: z.astype(F32)
    last = ()
    v = [dict() for _ in range(chunks)]
    m = {}
    at_end = (s == 0) | (s == nseq - 1)

    def after(*vals):
        if last:
            vals = lax.optimization_barrier(tuple(vals) + tuple(last))[:len(vals)]
        return vals

    def mark(*vals):
        nonlocal last
        last = vals

    def wait(d, *names):
        vals = after(*[d[n] for n in names])
        d.update(zip(names, vals))
        mark(*vals)

    def part(d, n, q):
        if f"y{n}{q}" in d:
            return d[f"y{n}{q}"]
        if not q:
            return jnp.concatenate([d[f"y{n}p"], d[f"y{n}q"]])
        half = d[f"y{n}"].shape[0] // 2
        return d[f"y{n}"][:half] if q == "p" else d[f"y{n}"][half:]

    def named():
        ids = jnp.arange(nblocks, dtype=jnp.int32)
        pos = jnp.sum(jnp.where(active[:, :, None] == ids, placement_map, 0), axis=2)
        m["n0"] = pos
        for k in range(1, nseq):
            m[f"n{k}"] = pp(pos, "seq", [(i, (i + k) % nseq) for i in range(nseq)])
        wait(m, *[f"n{k}" for k in range(1, nseq)])
        m["pos"] = jnp.stack([m[f"n{k}"] for k in range(nseq)])

    def setup():
        ew, dw = after(enc_weight, dec_weight)
        m["ep"] = pp(ew, "lat", SWAP)
        m["dp"] = pp(dw, "lat", SWAP)
        m["bo"] = enc_bias[None, :]
        m["bp"] = pp(m["bo"], "lat", SWAP)
        at = jnp.array([[0, 1, 2, 3], [1, 2, 3, 0], [2, 1, 0, 3], [3, 2, 1, 0]], jnp.int32)
        m["scal"] = jnp.concatenate([jnp.stack([at_end.astype(jnp.int32), (s * nlat + l) * local_blocks,
                                                (s * nlat + 1 - l) * local_blocks]), lax.rem(s - at[s] + nseq, nseq)])

    def step(name, c):
        d = v[c]
        if name == "x":
            (x,) = after(tokens[offs[c]:offs[c] + sizes[c]])
            d["x"] = (f32(x) - dec_bias[None, :]).astype(BF)
            mark(d["x"])
        elif name == "all":
            d["a1"] = d["c1"] = pp(after(d["x"])[0], "seq", TO_MID + TO_END)
        elif name == "setup":
            setup()
        elif name == "wset":
            wait(m, "ep", "dp", "bp")
        elif name == "named":
            named()
        elif name == "a1":
            d["a1"] = pp(after(d["x"])[0], "seq", TO_MID)
        elif name == "b1":
            d["b1"] = pp(after(d["x"])[0], "seq", ACROSS)
        elif name == "c1":
            d["c1"] = pp(after(d["x"])[0], "seq", TO_END)
        elif name == "b2":
            wait(d, "a1")
            d["b2"] = pp(d["a1"], "seq", ACROSS)
        elif name == "c2":
            wait(d, "b1")
            d["c2"] = pp(d["b1"], "seq", TO_END)
        elif name == "c3":
            wait(d, "b2")
            d["c3"] = pp(d["b2"], "seq", TO_END)
        elif name[:2] == "wx":
            wait(d, *["p" + name[2] + n for n in (("d", "x", "y") if name[2] in DIRECT else ("y",))])
        elif name[0] == "w":
            wait(d, name[1:])
        elif name[:2] == "en":
            h = name[2]
            ends, mids, slots, _ = GROUPS[h]
            rows = after(*[d[n] for n in ends + mids])
            pb = encode(m["scal"], m["pos"], offs[c], slots, rows[:len(ends)], rows[len(ends):], enc_weight, m["ep"], bw)
            mark(pb)
            d["p" + h] = pb
            if h in DIRECT:
                for n, p in (("d", FAR_TP), ("x", X_TP), ("y", Y_TP)):
                    d["p" + h + n] = pp(pb, "tp", p)
            else:
                d["p" + h + "x"] = pp(pb, "tp", X_TP)
        elif name[0] == "m":
            h = name[1]
            wait(d, "p" + h + "x")
            d["p" + h] = (f32(d["p" + h]) + f32(d["p" + h + "x"])).astype(BF)
            mark(d["p" + h])
            d["p" + h + "y"] = pp(d["p" + h], "tp", Y_TP)
        elif name[:2] == "de":
            h = name[2]
            parts = after(*[d["p" + h + n] for n in (("", "x", "y", "d") if h in DIRECT else ("", "y"))])
            _, _, slots, ys = GROUPS[h]
            kinds = [F32 if n == 0 else BF for n in slots]
            out = decode(m["scal"], m["pos"], offs[c], slots, kinds, parts, m["bo"], m["bp"], dec_weight, m["dp"],
                         len(ys) // len(slots))
            mark(*out)
            d.update(zip(ys, out))
        elif name[0] == "s":
            d[name] = pp(after(part(d, name[1], name[2:]))[0], "seq", TO_MID)
        elif name[0] in "tu":
            n, q = name[1], name[2:]
            src = ("s3" if n == "2" else "s2") if name[0] == "t" else "t2"
            wait(d, src + q)
            y = part(d, n if name[0] == "t" else "3", q)
            z = (f32(y) + f32(d[src + q])).astype(BF)
            mark(z)
            d[name] = pp(z, "seq", ACROSS if name[0] == "t" else TO_END)
        elif name == "fin":
            got = [[n] if n in d else [n + "p", n + "q"] for n in ("s1", "t1", "u1")]
            wait(d, *sum(got, []))
            s1, t1, u1 = [jnp.concatenate([f32(d[n]) for n in g]) for g in got]
            d["out"] = (d["y0"] + (s1 + t1 + u1) + dec_bias[None, :]).astype(BF)
            mark(d["out"])
        else:
            raise ValueError(name)

    for item in ORDER:
        name, c = item.split(".")
        step(name, int(c))
    return jnp.concatenate([d["out"] for d in v])


def general(tokens, active, placement_map, enc_weight, enc_bias, dec_weight, dec_bias):
    rows, width = tokens.shape
    top = active.shape[1]
    nblocks = placement_map.shape[0]
    seq_count = lax.axis_size("seq")
    lat_count = lax.axis_size("lat")
    owners = seq_count * lat_count
    local_blocks = nblocks // owners
    block_width = enc_bias.shape[0] // local_blocks
    capacity = 3 * rows * top // (2 * nblocks)
    centered = (tokens.astype(jnp.float32) - dec_bias[None, :]).astype(jnp.bfloat16)
    block_ids = jnp.arange(nblocks, dtype=jnp.int32)
    matches = (active[:, :, None] == block_ids[None, None, :]).astype(jnp.int32)
    position = jnp.sum(matches * placement_map[None, None, :], axis=2).reshape(-1)
    pos_hot = (position[:, None] == block_ids[None, :]).astype(jnp.int32)
    rank = jnp.sum((jnp.cumsum(pos_hot, axis=0) - 1) * pos_hot, axis=1)
    target = position * capacity + rank
    pair_row = jnp.arange(rows * top, dtype=jnp.int32) // top
    slot_row = jnp.zeros((nblocks * capacity,), jnp.int32).at[target].set(pair_row)
    filled = jnp.zeros((nblocks * capacity,), jnp.bool_).at[target].set(True)
    outgoing = jnp.where(filled[:, None], centered[slot_row], jnp.zeros((), jnp.bfloat16))
    outgoing = outgoing.reshape(owners, local_blocks, capacity, width)
    enc_blocks = enc_weight.reshape(width, local_blocks, block_width)
    bias_blocks = enc_bias.reshape(local_blocks, block_width)
    dec_blocks = dec_weight.reshape(local_blocks, block_width, width)
    preact = jnp.einsum(
        "sbcd,dbh->sbch",
        lax.all_to_all(outgoing, ("seq", "lat"), split_axis=0, concat_axis=0, tiled=True),
        enc_blocks,
        preferred_element_type=jnp.float32,
    )
    summed = lax.psum(preact, "tp")
    codes = jnp.maximum(summed + bias_blocks[None, :, None, :], 0.0).astype(jnp.bfloat16)
    returned = lax.all_to_all(
        jnp.einsum("sbch,bhd->sbcd", codes, dec_blocks, preferred_element_type=jnp.float32).astype(
            jnp.bfloat16
        ),
        ("seq", "lat"),
        split_axis=0,
        concat_axis=0,
        tiled=True,
    )
    returned = returned.reshape(nblocks * capacity, width)
    contrib = returned[target].reshape(rows, top, width).astype(jnp.float32)
    return (jnp.sum(contrib, axis=1) + dec_bias[None, :]).astype(jnp.bfloat16)


def solution(mesh):
    return jax.shard_map(
        line if dict(mesh.shape) == {"seq": 4, "tp": 4, "lat": 2} else general,
        mesh=mesh,
        in_specs=(
            P(("seq", "lat"), "tp"),
            P(("seq", "lat"), None),
            P(),
            P("tp", ("seq", "lat")),
            P(("seq", "lat")),
            P(("seq", "lat"), "tp"),
            P("tp"),
        ),
        out_specs=P(("seq", "lat"), "tp"),
        check_vma=False,
    )
```

```python
import jax
import jax.numpy as jnp
from jax import lax
from jax.experimental import pallas as pl
from jax.experimental.pallas import tpu as pltpu
from jax.sharding import PartitionSpec as P

SIXTHS = (12, 12)
DIRECT = ''
SPLIT = 'f'
ORDER = (
    "x.0", "all.0", "b1.0", "x.1", "named.0", "wa1.0", "wb1.0", "b2.0", "c2.0", "setup.0", "wset.0",
    "a1.1", "b1.1", "ena.0", "c3.0", "wc2.0", "ma.0", "b2.1", "c1.1", "dea.0", "s1.0", "c2.1",
    "wc3.0", "enb.0", "mb.0", "wc1.1", "ena.1", "ws1.0", "c3.1", "deb.0", "s3.0", "s2.0", "wc2.1",
    "ma.1", "dea.1", "s1.1", "t2.0", "wc3.1", "enf.1", "t1.0", "u1.0", "mf.1", "wxf.1", "def.1",
    "s3p.1", "s3q.1", "s2p.1", "s2q.1", "ws1.1", "fin.0", "t2p.1", "t2q.1", "t1p.1", "u1p.1",
    "t1q.1", "u1q.1", "fin.1",
)
TO_MID = [(0, 1), (3, 2)]
ACROSS = [(1, 2), (2, 1)]
TO_END = [(1, 0), (2, 3)]
SWAP = [(0, 1), (1, 0)]
X_TP, Y_TP, FAR_TP = [(0, 1), (1, 0), (2, 3), (3, 2)], [(0, 2), (2, 0), (1, 3), (3, 1)], [(0, 3), (3, 0), (1, 2), (2, 1)]
BF = jnp.bfloat16
F32 = jnp.float32
WSPEC = pl.BlockSpec(memory_space=pltpu.VMEM)
VMEM = 20 << 20
DTILE = 1024


def encode_kernel(slots, off, s_ref, pos, *refs):
    half = len(slots)
    at_end, at_mid = refs[:half], refs[half:2 * half]
    wo, wp, outs, (xs, pre, sem) = refs[2 * half], refs[2 * half + 1], refs[2 * half + 2:-3], refs[-3:]
    r = xs.shape[0] // half
    top = pos.shape[2]
    bw = outs[0].shape[1] // top
    cols = wo.shape[1]
    end = s_ref[0] == 1

    def move(i, src):
        return pltpu.make_async_copy(src, xs.at[i * r:(i + 1) * r], sem.at[i])

    @pl.when(end)
    def _():
        for i, src in enumerate(at_end):
            move(i, src).start()

    @pl.when(jnp.logical_not(end))
    def _():
        for i, src in enumerate(at_mid):
            move(i, src).start()

    for i in range(half):
        move(i, at_end[i]).wait()
    pre[:, :cols] = jnp.dot(xs[...], wo[...], preferred_element_type=F32)
    pre[:, cols:] = jnp.dot(xs[...], wp[...], preferred_element_type=F32)
    step = next(n for n in (64, 48, 32, 16) if r % n == 0)
    for i, slot in enumerate(slots):
        for at in range(0, r, step):
            p = pos[s_ref[3 + slot], off + at:off + at + step, :]
            rs = slice(i * r + at, i * r + at + step)
            for k in range(top):
                q = jnp.broadcast_to(p[:, k:k + 1], (step, bw))
                a = jnp.zeros((step, bw), F32)
                for b in range(2 * cols // bw):
                    base = s_ref[1] + b if b < cols // bw else s_ref[2] + b - cols // bw
                    a = jnp.where(q == base, pre[rs, b * bw:(b + 1) * bw], a)
                if len(outs) == 1:
                    outs[0][rs, k * bw:(k + 1) * bw] = a.astype(BF)
                else:
                    outs[i][at:at + step, k * bw:(k + 1) * bw] = a.astype(BF)


def decode_kernel(slots, off, count, split, s_ref, pos, *refs):
    parts, (bo, bp, wo, wp), outs, codes = refs[:count], refs[count:count + 4], refs[count + 4:-1], refs[-1]
    own = parts[0]
    top = pos.shape[2]
    bw = own.shape[1] // top
    r = own.shape[0] if split else own.shape[0] // len(slots)
    h, width = wo.shape
    for i, slot in enumerate(slots):
        p = pos[s_ref[3 + slot], off:off + r, :]
        rs = slice(i * r, (i + 1) * r)
        wide = [jnp.broadcast_to(p[:, k:k + 1], (r, bw)) for k in range(top)]
        mine = parts[i * count // len(slots):(i + 1) * count // len(slots)] if split else parts
        ps = slice(0, r) if split else rs
        tot = [sum(q[ps, c].astype(F32) for q in mine)
               for c in (slice(k * bw, (k + 1) * bw) for k in range(top))]
        for bias, base, at in ((bo, s_ref[1], 0), (bp, s_ref[2], h)):
            for b in range(h // bw):
                v = jnp.full((r, bw), -jnp.inf, F32)
                for k in range(top):
                    v = jnp.where(wide[k] == base + b, tot[k], v)
                codes[rs, at + b * bw:at + (b + 1) * bw] = jnp.maximum(v + bias[:, b * bw:(b + 1) * bw], 0.0).astype(BF)
    tile = DTILE
    for n in range(width // tile):
        c = slice(n * tile, (n + 1) * tile)
        y = jnp.dot(codes[:, :h], wo[:, c], preferred_element_type=F32) + jnp.dot(
            codes[:, h:], wp[:, c], preferred_element_type=F32)
        row = 0
        for o in outs:
            o[:, c] = y[row:row + o.shape[0]].astype(o.dtype)
            row += o.shape[0]


GROUPS = {
    "a": (("x", "c1"), ("x", "b1"), (0, 1), ("y0", "y1")),
    "b": (("c2", "c3"), ("b2", "a1"), (2, 3), ("y2", "y3")),
    "d": (("c2",), ("b2",), (2,), ("y2",)),
    "f": (("c2", "c3"), ("b2", "a1"), (2, 3), ("y2p", "y2q", "y3p", "y3q")),
    "e": (("c3",), ("a1",), (3,), ("y3p", "y3q")),
}
NEAR, FAR = pl.BlockSpec(memory_space=pltpu.VMEM), pl.BlockSpec(memory_space=pl.ANY)


def encode(scal, pos, off, slots, at_end, at_mid, wo, wp, bw, cut):
    r, width = at_end[0].shape
    cols = wo.shape[1]
    top = pos.shape[2]
    n = len(slots)
    return pl.pallas_call(
        lambda *refs: encode_kernel(slots, off, *refs),
        out_shape=[jax.ShapeDtypeStruct((n * r // cut, top * bw), BF)] * cut,
        in_specs=[pl.BlockSpec(memory_space=pltpu.SMEM), NEAR] + [FAR] * (2 * n) + [WSPEC] * 2,
        out_specs=[NEAR] * cut,
        scratch_shapes=[pltpu.VMEM((n * r, width), BF), pltpu.VMEM((n * r, 2 * cols), F32), pltpu.SemaphoreType.DMA((n,))],
        compiler_params=pltpu.CompilerParams(vmem_limit_bytes=VMEM),
        cost_estimate=pl.CostEstimate(flops=1, bytes_accessed=1, transcendentals=0),
        name="encode",
    )(scal, pos, *at_end, *at_mid, wo, wp)


def decode(scal, pos, off, slots, kinds, parts, bo, bp, wo, wp, cut, split):
    n = len(slots)
    r = parts[0].shape[0] if split else parts[0].shape[0] // n
    half, width = wo.shape
    return pl.pallas_call(
        lambda *refs: decode_kernel(slots, off, len(parts), split, *refs),
        out_shape=[jax.ShapeDtypeStruct((r // cut, width), kind) for kind in kinds for _ in range(cut)],
        in_specs=[pl.BlockSpec(memory_space=pltpu.SMEM)] + [NEAR] * (3 + len(parts)) + [WSPEC] * 2,
        out_specs=[NEAR] * (len(kinds) * cut),
        scratch_shapes=[pltpu.VMEM((n * r, 2 * half), BF)],
        compiler_params=pltpu.CompilerParams(vmem_limit_bytes=VMEM),
        cost_estimate=pl.CostEstimate(flops=1, bytes_accessed=1, transcendentals=0),
        name="decode",
    )(scal, pos, *parts, bo, bp, wo, wp)


def line(tokens, active, placement_map, enc_weight, enc_bias, dec_weight, dec_bias):
    rows, width = tokens.shape
    nblocks = placement_map.shape[0]
    nseq, nlat = lax.axis_size("seq"), lax.axis_size("lat")
    local_blocks = nblocks // (nseq * nlat)
    bw = enc_bias.shape[0] // local_blocks
    s, l = lax.axis_index("seq"), lax.axis_index("lat")
    chunks = len(SIXTHS)
    sizes = [rows * n // sum(SIXTHS) for n in SIXTHS]
    offs = [sum(sizes[:c]) for c in range(chunks)]
    pp = lax.ppermute
    f32 = lambda z: z.astype(F32)
    last = ()
    v = [dict() for _ in range(chunks)]
    m = {}
    at_end = (s == 0) | (s == nseq - 1)

    def after(*vals):
        if last:
            vals = lax.optimization_barrier(tuple(vals) + tuple(last))[:len(vals)]
        return vals

    def mark(*vals):
        nonlocal last
        last = vals

    def wait(d, *names):
        vals = after(*[d[n] for n in names])
        d.update(zip(names, vals))
        mark(*vals)

    def part(d, n, q):
        if f"y{n}{q}" in d:
            return d[f"y{n}{q}"]
        if not q:
            return jnp.concatenate([d[f"y{n}p"], d[f"y{n}q"]])
        half = d[f"y{n}"].shape[0] // 2
        return d[f"y{n}"][:half] if q == "p" else d[f"y{n}"][half:]

    def named():
        ids = jnp.arange(nblocks, dtype=jnp.int32)
        pos = jnp.sum(jnp.where(active[:, :, None] == ids, placement_map, 0), axis=2)
        m["n0"] = pos
        for k in range(1, nseq):
            m[f"n{k}"] = pp(pos, "seq", [(i, (i + k) % nseq) for i in range(nseq)])
        wait(m, *[f"n{k}" for k in range(1, nseq)])
        m["pos"] = jnp.stack([m[f"n{k}"] for k in range(nseq)])

    def setup():
        ew, dw = after(enc_weight, dec_weight)
        m["ep"] = pp(ew, "lat", SWAP)
        m["dp"] = pp(dw, "lat", SWAP)
        m["bo"] = enc_bias[None, :]
        m["bp"] = pp(m["bo"], "lat", SWAP)
        at = jnp.array([[0, 1, 2, 3], [1, 2, 3, 0], [2, 1, 0, 3], [3, 2, 1, 0]], jnp.int32)
        m["scal"] = jnp.concatenate([jnp.stack([at_end.astype(jnp.int32), (s * nlat + l) * local_blocks,
                                                (s * nlat + 1 - l) * local_blocks]), lax.rem(s - at[s] + nseq, nseq)])

    def step(name, c):
        d = v[c]
        if name == "x":
            (x,) = after(tokens[offs[c]:offs[c] + sizes[c]])
            d["x"] = (f32(x) - dec_bias[None, :]).astype(BF)
            mark(d["x"])
        elif name == "all":
            d["a1"] = d["c1"] = pp(after(d["x"])[0], "seq", TO_MID + TO_END)
        elif name == "setup":
            setup()
        elif name == "wset":
            wait(m, "ep", "dp", "bp")
        elif name == "named":
            named()
        elif name == "a1":
            d["a1"] = pp(after(d["x"])[0], "seq", TO_MID)
        elif name == "b1":
            d["b1"] = pp(after(d["x"])[0], "seq", ACROSS)
        elif name == "c1":
            d["c1"] = pp(after(d["x"])[0], "seq", TO_END)
        elif name == "b2":
            wait(d, "a1")
            d["b2"] = pp(d["a1"], "seq", ACROSS)
        elif name == "c2":
            wait(d, "b1")
            d["c2"] = pp(d["b1"], "seq", TO_END)
        elif name == "c3":
            wait(d, "b2")
            d["c3"] = pp(d["b2"], "seq", TO_END)
        elif name[:2] == "wx":
            h = name[2]
            wait(d, *(("r" + h + "x", "r" + h + "y") if h in SPLIT else ["p" + h + n for n in (("d", "x", "y") if h in DIRECT else ("y",))]))
        elif name[0] == "w":
            wait(d, name[1:])
        elif name[:2] == "en":
            h = name[2]
            ends, mids, slots, _ = GROUPS[h]
            rows = after(*[d[n] for n in ends + mids])
            pb = encode(m["scal"], m["pos"], offs[c], slots, rows[:len(ends)], rows[len(ends):], enc_weight, m["ep"], bw,
                        2 if h in SPLIT else 1)
            mark(*pb)
            if h in SPLIT:
                for n, p, q in zip("xy", pb, (X_TP, Y_TP)):
                    d["q" + h + n], d["r" + h + n] = p, pp(p, "tp", q)
                return
            pb = d["p" + h] = pb[0]
            if h in DIRECT:
                for n, p in (("d", FAR_TP), ("x", X_TP), ("y", Y_TP)):
                    d["p" + h + n] = pp(pb, "tp", p)
            else:
                d["p" + h + "x"] = pp(pb, "tp", X_TP)
        elif name[0] == "m":
            h = name[1]
            if h in SPLIT:
                wait(d, "r" + h + "x", "r" + h + "y")
                for n in "xy":
                    d["q" + h + n] = (f32(d["q" + h + n]) + f32(d["r" + h + n])).astype(BF)
                mark(d["q" + h + "x"], d["q" + h + "y"])
                for n, q in zip("xy", (Y_TP, X_TP)):
                    d["r" + h + n] = pp(d["q" + h + n], "tp", q)
                return
            wait(d, "p" + h + "x")
            d["p" + h] = (f32(d["p" + h]) + f32(d["p" + h + "x"])).astype(BF)
            mark(d["p" + h])
            d["p" + h + "y"] = pp(d["p" + h], "tp", Y_TP)
        elif name[:2] == "de":
            h = name[2]
            names = ["p" + h + n for n in (("", "x", "y", "d") if h in DIRECT else ("", "y"))]
            if h in SPLIT:
                names = [k + h + n for n in "xy" for k in "qr"]
            parts = after(*[d[n] for n in names])
            _, _, slots, ys = GROUPS[h]
            kinds = [F32 if n == 0 else BF for n in slots]
            out = decode(m["scal"], m["pos"], offs[c], slots, kinds, parts, m["bo"], m["bp"], dec_weight, m["dp"],
                         len(ys) // len(slots), h in SPLIT)
            mark(*out)
            d.update(zip(ys, out))
        elif name[0] == "s":
            d[name] = pp(after(part(d, name[1], name[2:]))[0], "seq", TO_MID)
        elif name[0] in "tu":
            n, q = name[1], name[2:]
            src = ("s3" if n == "2" else "s2") if name[0] == "t" else "t2"
            wait(d, src + q)
            y = part(d, n if name[0] == "t" else "3", q)
            z = (f32(y) + f32(d[src + q])).astype(BF)
            mark(z)
            d[name] = pp(z, "seq", ACROSS if name[0] == "t" else TO_END)
        elif name == "fin":
            got = [[n] if n in d else [n + "p", n + "q"] for n in ("s1", "t1", "u1")]
            wait(d, *sum(got, []))
            s1, t1, u1 = [jnp.concatenate([f32(d[n]) for n in g]) for g in got]
            d["out"] = (d["y0"] + (s1 + t1 + u1) + dec_bias[None, :]).astype(BF)
            mark(d["out"])
        else:
            raise ValueError(name)

    for item in ORDER:
        name, c = item.split(".")
        step(name, int(c))
    return jnp.concatenate([d["out"] for d in v])


def general(tokens, active, placement_map, enc_weight, enc_bias, dec_weight, dec_bias):
    rows, width = tokens.shape
    top = active.shape[1]
    nblocks = placement_map.shape[0]
    seq_count = lax.axis_size("seq")
    lat_count = lax.axis_size("lat")
    owners = seq_count * lat_count
    local_blocks = nblocks // owners
    block_width = enc_bias.shape[0] // local_blocks
    capacity = 3 * rows * top // (2 * nblocks)
    centered = (tokens.astype(jnp.float32) - dec_bias[None, :]).astype(jnp.bfloat16)
    block_ids = jnp.arange(nblocks, dtype=jnp.int32)
    matches = (active[:, :, None] == block_ids[None, None, :]).astype(jnp.int32)
    position = jnp.sum(matches * placement_map[None, None, :], axis=2).reshape(-1)
    pos_hot = (position[:, None] == block_ids[None, :]).astype(jnp.int32)
    rank = jnp.sum((jnp.cumsum(pos_hot, axis=0) - 1) * pos_hot, axis=1)
    target = position * capacity + rank
    pair_row = jnp.arange(rows * top, dtype=jnp.int32) // top
    slot_row = jnp.zeros((nblocks * capacity,), jnp.int32).at[target].set(pair_row)
    filled = jnp.zeros((nblocks * capacity,), jnp.bool_).at[target].set(True)
    outgoing = jnp.where(filled[:, None], centered[slot_row], jnp.zeros((), jnp.bfloat16))
    outgoing = outgoing.reshape(owners, local_blocks, capacity, width)
    enc_blocks = enc_weight.reshape(width, local_blocks, block_width)
    bias_blocks = enc_bias.reshape(local_blocks, block_width)
    dec_blocks = dec_weight.reshape(local_blocks, block_width, width)
    preact = jnp.einsum(
        "sbcd,dbh->sbch",
        lax.all_to_all(outgoing, ("seq", "lat"), split_axis=0, concat_axis=0, tiled=True),
        enc_blocks,
        preferred_element_type=jnp.float32,
    )
    summed = lax.psum(preact, "tp")
    codes = jnp.maximum(summed + bias_blocks[None, :, None, :], 0.0).astype(jnp.bfloat16)
    returned = lax.all_to_all(
        jnp.einsum("sbch,bhd->sbcd", codes, dec_blocks, preferred_element_type=jnp.float32).astype(
            jnp.bfloat16
        ),
        ("seq", "lat"),
        split_axis=0,
        concat_axis=0,
        tiled=True,
    )
    returned = returned.reshape(nblocks * capacity, width)
    contrib = returned[target].reshape(rows, top, width).astype(jnp.float32)
    return (jnp.sum(contrib, axis=1) + dec_bias[None, :]).astype(jnp.bfloat16)


def solution(mesh):
    return jax.shard_map(
        line if dict(mesh.shape) == {"seq": 4, "tp": 4, "lat": 2} else general,
        mesh=mesh,
        in_specs=(
            P(("seq", "lat"), "tp"),
            P(("seq", "lat"), None),
            P(),
            P("tp", ("seq", "lat")),
            P(("seq", "lat")),
            P(("seq", "lat"), "tp"),
            P("tp"),
        ),
        out_specs=P(("seq", "lat"), "tp"),
        check_vma=False,
    )
```
